32 devices in a mesh: replica: 8 (over z, y), fsdp: 4 (over x, core).
Axes of the slice: x: 2, y: 2, z: 4, core: 2. Of those that a mesh axis runs over, the one named last changes fastest.
Arguments:
- tokens_in: bfloat16 [8, 1024, 1088], P('replica', 'fsdp'), may hold values from -6 to 6
- norm1_gain: bfloat16 [1088], P('fsdp'), may hold values from 0.099609375 to 1.8984375
- norm1_bias: bfloat16 [1088], P('fsdp'), may hold values from -3 to 3
- qkv_weight: bfloat16 [1088, 3264], P('fsdp'), may hold values from -0.1875 to 0.1875
- query_bias: bfloat16 [1088], P('fsdp'), may hold values from -3 to 3
- value_bias: bfloat16 [1088], P('fsdp'), may hold values from -3 to 3
- out_weight: bfloat16 [1088, 1088], P('fsdp'), may hold values from -1.5 to 1.5
- out_bias: bfloat16 [1088], P('fsdp'), may hold values from -3 to 3
- norm2_gain: bfloat16 [1088], P('fsdp'), may hold values from 0.099609375 to 1.8984375
- norm2_bias: bfloat16 [1088], P('fsdp'), may hold values from -3 to 3
- up_weight: bfloat16 [1088, 4352], P('fsdp'), may hold values from -0.1875 to 0.1875
- up_bias: bfloat16 [4352], P('fsdp'), may hold values from -3 to 3
- down_weight: bfloat16 [4352, 1088], P('fsdp'), may hold values from -0.09375 to 0.09375
- down_bias: bfloat16 [1088], P('fsdp'), may hold values from -3 to 3
- out_grad: bfloat16 [8, 1024, 1088], P('replica', 'fsdp'), may hold values from -6 to 6
Outputs:
- block_out: bfloat16 [8, 1024, 1088], P('replica', 'fsdp')
- input_grad: float32 [8, 1024, 1088], P('replica', 'fsdp')
- grad_norm1_gain: float32 [1088], P('fsdp')
- grad_norm1_bias: float32 [1088], P('fsdp')
- grad_qkv_weight: float32 [1088, 3264], P('fsdp')
- grad_query_bias: float32 [1088], P('fsdp')
- grad_value_bias: float32 [1088], P('fsdp')
- grad_out_weight: float32 [1088, 1088], P('fsdp')
- grad_out_bias: float32 [1088], P('fsdp')
- grad_norm2_gain: float32 [1088], P('fsdp')
- grad_norm2_bias: float32 [1088], P('fsdp')
- grad_up_weight: float32 [1088, 4352], P('fsdp')
- grad_up_bias: float32 [4352], P('fsdp')
- grad_down_weight: float32 [4352, 1088], P('fsdp')
- grad_down_bias: float32 [1088], P('fsdp')
The draws below stay inside these ranges and needn't reach their ends.
All inputs are finite; a program needn't handle non-finite values.
Results may differ from the reference program's by a relative error of at most 0.019.
Values may be sent and summed in bfloat16 or wider, within the bound.
A program may use at most 256 MiB of HBM per device.

```python
import math
import jax
import jax.numpy as jnp
from jax import lax

D = 1088
HEADS = 17
HEAD_DIM = 64
FF = 4352
LENGTH = 1024
SEQ_TOTAL = 8


def levels(key, dims, split, least, high):
    loudness = 1.0
    for position, shards_of in split:
        draws = jax.random.uniform(jax.random.fold_in(jax.random.fold_in(key, 6), position), (shards_of,), jnp.float32, least / len(split), high / len(split))
        loudness = loudness * jnp.repeat(jnp.exp(draws), dims[position] // shards_of).reshape((-1,) + (1,) * (len(dims) - 1 - position))
    return loudness


def normal_values(key, dims, deviation, bound, cuts=(), kind=jnp.bfloat16):
    array = jax.random.normal(key, dims, jnp.float32) * deviation
    if len(cuts) > 0:
        array = levels(key, dims, cuts, -0.22, 0.18) * array
    return jnp.clip(array, min=-bound, max=bound).astype(kind)


def setup_inputs(seed: int = 0) -> dict:
    keys = jax.random.split(jax.random.key(seed), 16)
    tokens_in = normal_values(keys[0], (SEQ_TOTAL, LENGTH, D), 1.0, 6.0, ((0, 8), (1, 4)))
    norm1_gain = jnp.clip(1.0 + 0.18 * jax.random.normal(keys[1], (D,), jnp.float32), 0.099609375, 1.8984375).astype(jnp.bfloat16)
    norm1_bias = normal_values(keys[2], (D,), 0.5, 3.0, ((0, 4),))
    qkv_weight = normal_values(keys[3], (D, 3 * D), D ** -0.5, 0.1875, ((0, 4),))
    query_bias = normal_values(keys[4], (D,), 0.5, 3.0, ((0, 4),))
    value_bias = normal_values(keys[5], (D,), 0.5, 3.0, ((0, 4),))
    out_weight = normal_values(keys[6], (D, D), (max(1, D // 64)) ** -0.5, 1.5, ((0, 4),))
    out_bias = normal_values(keys[7], (D,), 0.5, 3.0, ((0, 4),))
    norm2_gain = jnp.clip(1.0 + 0.18 * jax.random.normal(keys[8], (D,), jnp.float32), 0.099609375, 1.8984375).astype(jnp.bfloat16)
    norm2_bias = normal_values(keys[9], (D,), 0.5, 3.0, ((0, 4),))
    up_weight = normal_values(keys[10], (D, FF), D ** -0.5, 0.1875, ((0, 4),))
    up_bias = normal_values(keys[11], (FF,), 0.5, 3.0, ((0, 4),))
    down_weight = normal_values(keys[12], (FF, D), FF ** -0.5, 0.09375, ((0, 4),))
    down_bias = normal_values(keys[13], (D,), 0.5, 3.0, ((0, 4),))
    out_grad = normal_values(keys[14], (SEQ_TOTAL, LENGTH, D), 1.0, 6.0, ((0, 8), (1, 4)))
    return {"tokens_in": tokens_in, "norm1_gain": norm1_gain, "norm1_bias": norm1_bias, "qkv_weight": qkv_weight, "query_bias": query_bias, "value_bias": value_bias, "out_weight": out_weight, "out_bias": out_bias, "norm2_gain": norm2_gain, "norm2_bias": norm2_bias, "up_weight": up_weight, "up_bias": up_bias, "down_weight": down_weight, "down_bias": down_bias, "out_grad": out_grad}


EPSILON = 1e-05
MASKED = -1e+30
EXACT = lax.Precision.HIGHEST

@jax.custom_vjp
def low(v):
    return lax.optimization_barrier(v.astype(jnp.bfloat16)).astype(jnp.float32)

@jax.custom_vjp
def low_back(v):
    return v

def low_keep(v):
    return (low(v), None)

def low_pass(kept, grad):
    return (grad,)

def back_keep(v):
    return (v, None)

def back_low(kept, grad):
    return (low(grad),)
low.defvjp(low_keep, low_pass)
low_back.defvjp(back_keep, back_low)

def norm_rows(values, gain, shift):
    center = values - lax.optimization_barrier(jnp.mean(values, axis=-1, keepdims=True))
    spread = lax.optimization_barrier(jnp.mean(center * center, axis=-1, keepdims=True))
    return center * lax.rsqrt(spread + EPSILON) * gain + shift

def gelu_exact(values):
    return 0.5 * values * (1.0 + jax.scipy.special.erf(values * (1.0 / math.sqrt(2.0))))

def attend(queries, key_rows, value_rows):
    row_block = min(512, LENGTH)
    blocks = LENGTH // row_block
    key_index = jnp.arange(LENGTH, dtype=jnp.int32)
    factor = 1.0 / math.sqrt(HEAD_DIM)

    def query_block(inputs):
        block_rows, offset = inputs
        raw_scores = jnp.einsum('qhe,khe->hqk', block_rows, key_rows, precision=EXACT)
        scores = low_back(factor * raw_scores)
        row_index = offset + jnp.arange(row_block, dtype=jnp.int32)
        allowed = key_index[None, :] <= row_index[:, None]
        scores = jnp.where(allowed[None], scores, MASKED)
        highest = lax.optimization_barrier(jnp.max(scores, axis=-1, keepdims=True))
        weights = jnp.exp(scores - highest)
        attention = weights / lax.optimization_barrier(jnp.sum(weights, axis=-1, keepdims=True))
        return jnp.einsum('hqk,khe->qhe', low(attention), value_rows, precision=EXACT)
    offsets = jnp.arange(blocks, dtype=jnp.int32) * row_block
    stacked = lax.map(jax.checkpoint(query_block), (queries.reshape(blocks, row_block, HEADS, HEAD_DIM), offsets))
    return stacked.reshape(LENGTH, D)

def block_layer(tokens, params):
    norm1_gain, norm1_bias, qkv_weight, query_bias, value_bias, out_weight, out_bias, norm2_gain, norm2_bias, up_weight, up_bias, down_weight, down_bias = params
    normed = low(norm_rows(tokens, norm1_gain, norm1_bias))
    biases = jnp.concatenate([query_bias, jnp.zeros_like(query_bias), value_bias])
    projected = low(low_back(jnp.dot(normed, qkv_weight, precision=EXACT) + biases))
    queries = projected[:, :D].reshape(LENGTH, HEADS, HEAD_DIM)
    key_rows = projected[:, D:2 * D].reshape(LENGTH, HEADS, HEAD_DIM)
    value_rows = projected[:, 2 * D:].reshape(LENGTH, HEADS, HEAD_DIM)
    attended = low(low_back(attend(queries, key_rows, value_rows)))
    middle = tokens + low_back(jnp.dot(attended, out_weight, precision=EXACT) + out_bias)
    second = low(norm_rows(middle, norm2_gain, norm2_bias))
    hidden = low(gelu_exact(low_back(jnp.dot(second, up_weight, precision=EXACT) + up_bias)))
    return middle + jnp.dot(hidden, down_weight, precision=EXACT) + down_bias

def reference(tokens_in, norm1_gain, norm1_bias, qkv_weight, query_bias, value_bias, out_weight, out_bias, norm2_gain, norm2_bias, up_weight, up_bias, down_weight, down_bias, out_grad):
    params = tuple((argument.astype(jnp.float32) for argument in (norm1_gain, norm1_bias, qkv_weight, query_bias, value_bias, out_weight, out_bias, norm2_gain, norm2_bias, up_weight, up_bias, down_weight, down_bias)))

    def whole_batch(inputs, weights):

        def per_sequence(carried, tokens):
            return (carried, jax.checkpoint(block_layer)(tokens, weights))
        unused_carry, results = lax.scan(per_sequence, jnp.zeros((), jnp.float32), inputs)
        return results
    results, pullback = jax.vjp(whole_batch, tokens_in.astype(jnp.float32), params)
    grad_tokens, gradients = pullback(out_grad.astype(jnp.float32))
    return (results.astype(jnp.bfloat16), grad_tokens, gradients[0], gradients[1], gradients[2], gradients[3], gradients[4], gradients[5], gradients[6], gradients[7], gradients[8], gradients[9], gradients[10], gradients[11], gradients[12])
```

```python
import functools
import math

import jax
import jax.numpy as jnp
from jax import lax
from jax.sharding import PartitionSpec as P

HEADS = 17
HEAD_DIM = 64


EPSILON = 1e-05
MASKED = -1e30
SWAP = ((0, 1), (1, 0))
NEAR = ((0, 1), (1, 0), (2, 3), (3, 2))
FAR = ((0, 2), (2, 0), (1, 3), (3, 1))


def norm_rows(values, gain, shift):
    center = values - jnp.mean(values, axis=-1, keepdims=True)
    inverse = lax.rsqrt(jnp.mean(center * center, axis=-1, keepdims=True) + EPSILON)
    scaled = center * inverse
    return (scaled, inverse, scaled * gain + shift)


def norm_back(upstream, scaled, inverse, gain):
    weighted = upstream * gain
    inner = (
        weighted
        - jnp.mean(weighted, axis=-1, keepdims=True)
        - scaled * jnp.mean(weighted * scaled, axis=-1, keepdims=True)
    )
    return (inverse * inner, jnp.sum(upstream * scaled, axis=0), jnp.sum(upstream, axis=0))


def gelu_exact(values):
    return 0.5 * values * (1.0 + jax.scipy.special.erf(values * (1.0 / math.sqrt(2.0))))


def masked_scores(row_heads, key_heads, row_index, key_index, factor):
    raw_scores = jnp.einsum(
        "sqhe,skhe->shqk", row_heads, key_heads, preferred_element_type=jnp.float32
    )
    allowed = key_index[None, :] <= row_index[:, None]
    return jnp.where(allowed[None, None], raw_scores * factor, MASKED)


def pair_terms(
    row_heads,
    grad_heads,
    key_heads,
    value_heads,
    row_index,
    key_index,
    log_total,
    delta_rows,
    factor,
):
    scores = masked_scores(row_heads, key_heads, row_index, key_index, factor)
    probs_full = jnp.exp(scores - log_total[..., None])
    prob_grads = jnp.einsum(
        "sqhe,skhe->shqk", grad_heads, value_heads, preferred_element_type=jnp.float32
    )
    score_grads = (probs_full * (prob_grads - delta_rows[..., None])).astype(jnp.bfloat16)
    return (probs_full.astype(jnp.bfloat16), score_grads)


class AxisComm:
    group = "fsdp"
    sets = "replica"

    def gather(self, shard):
        return lax.all_gather(shard, "fsdp", axis=0, tiled=True)

    def reduce(self, local):
        owned = lax.psum_scatter(local, "fsdp", scatter_dimension=0, tiled=True)
        return lax.psum(owned, "replica").astype(jnp.float32)

    def reduce_small(self, packed):
        total = lax.psum(packed, ("replica", "fsdp"))
        return lax.dynamic_index_in_dim(total, lax.axis_index("fsdp"), 0, keepdims=False)

    def scatter_tokens(self, local):
        return lax.psum_scatter(local, "fsdp", scatter_dimension=1, tiled=True)


def split_half(rows):
    size = -(-rows // 16) * 8
    return (size, rows - size)


def halve(array, name, pairs, place):
    size, second = split_half(array.shape[0])
    keep = lax.dynamic_slice_in_dim(array, place * second, size, 0)
    send = lax.dynamic_slice_in_dim(array, (1 - place) * second, size, 0)
    got = lax.ppermute(send, name, pairs)
    return (keep.astype(jnp.float32) + got.astype(jnp.float32)).astype(array.dtype)


def join(array, name, pairs, place, rows):
    _, second = split_half(rows)
    got = lax.ppermute(array, name, pairs)
    low = jnp.where(place == 0, array, got)
    high = jnp.where(place == 0, got, array)
    return jnp.concatenate([low[:second], high], axis=0)


class TorusComm:
    group = ("x", "core")
    sets = ("z", "y")

    def gather(self, shard):
        x, y, core = (lax.axis_index(name) for name in ("x", "y", "core"))
        rows = shard.shape[0]
        beside = lax.ppermute(shard, "core", SWAP)
        if rows % 16 == 0:
            half = rows // 2
            piece = lax.dynamic_slice_in_dim(shard, y * half, half, 0)
            got = lax.ppermute(piece, "x", SWAP)
            other = lax.ppermute(got, "y", SWAP)
            far = jnp.concatenate(
                [jnp.where(y == 0, got, other), jnp.where(y == 0, other, got)], axis=0
            )
        else:
            far = lax.ppermute(shard, "x", SWAP)
        far_beside = lax.ppermute(far, "core", SWAP)
        near_first = jnp.where(core == 0, shard, beside)
        near_second = jnp.where(core == 0, beside, shard)
        far_first = jnp.where(core == 0, far, far_beside)
        far_second = jnp.where(core == 0, far_beside, far)
        return jnp.concatenate(
            [
                jnp.where(x == 0, near_first, far_first),
                jnp.where(x == 0, near_second, far_second),
                jnp.where(x == 0, far_first, near_first),
                jnp.where(x == 0, far_second, near_second),
            ],
            axis=0,
        )

    def scatter_group(self, blocks):
        x, core = lax.axis_index("x"), lax.axis_index("core")
        for name, place, dim in (("core", core, 1), ("x", x, 0)):
            keep = lax.dynamic_index_in_dim(blocks, place, dim, keepdims=False)
            send = lax.dynamic_index_in_dim(blocks, 1 - place, dim, keepdims=False)
            got = lax.ppermute(send, name, SWAP)
            blocks = (keep.astype(jnp.float32) + got.astype(jnp.float32)).astype(blocks.dtype)
        return blocks

    def reduce(self, local):
        y, z = lax.axis_index("y"), lax.axis_index("z")
        rows = local.shape[0] // 4
        own = self.scatter_group(local.reshape(2, 2, rows, local.shape[1]))
        steps = (("y", SWAP, y), ("z", NEAR, lax.rem(z, 2)), ("z", FAR, lax.div(z, 2)))
        sizes = []
        for name, pairs, place in steps:
            sizes.append(own.shape[0])
            own = halve(own, name, pairs, place)
        for (name, pairs, place), size in zip(steps[::-1], sizes[::-1]):
            own = join(own, name, pairs, place, size)
        return own.astype(jnp.float32)

    def reduce_small(self, packed):
        for name, pairs in (
            ("core", SWAP),
            ("x", SWAP),
            ("y", SWAP),
            ("z", NEAR),
            ("z", FAR),
        ):
            packed = packed + lax.ppermute(packed, name, pairs)
        place = lax.axis_index("x") * 2 + lax.axis_index("core")
        return lax.dynamic_index_in_dim(packed, place, 0, keepdims=False)

    def scatter_tokens(self, local):
        sequences, length, width = local.shape
        blocks = local.reshape(sequences, 2, 2, length // 4, width)
        return jax.vmap(self.scatter_group)(blocks)


def shards(
    comm,
    tokens_in,
    norm1_gain,
    norm1_bias,
    qkv_weight,
    query_bias,
    value_bias,
    out_weight,
    out_bias,
    norm2_gain,
    norm2_bias,
    up_weight,
    up_bias,
    down_weight,
    down_bias,
    out_grad,
):
    vectors = (
        norm1_gain,
        norm1_bias,
        query_bias,
        value_bias,
        out_bias,
        norm2_gain,
        norm2_bias,
        down_bias,
        up_bias,
    )
    members = lax.axis_size(comm.group)
    every = lax.all_gather(jnp.concatenate(vectors), comm.group, axis=0)
    pieces, position = [], 0
    for member in vectors:
        pieces.append(every[:, position : position + member.size].reshape(-1))
        position = position + member.size
    (
        first_gain,
        first_shift,
        query_shift,
        value_shift,
        out_shift,
        second_gain,
        second_shift,
        down_shift,
        up_shift,
    ) = pieces
    full_qkv = comm.gather(qkv_weight)
    full_out = comm.gather(out_weight)
    full_up = comm.gather(up_weight)
    full_down = comm.gather(down_weight)
    sequences, local_len, model_width = tokens_in.shape
    row_count = sequences * local_len
    device_index = lax.axis_index(comm.group)
    factor = 1.0 / math.sqrt(HEAD_DIM)
    inputs = tokens_in.astype(jnp.float32).reshape(row_count, model_width)
    scaled_one, inverse_one, normed_one = norm_rows(
        inputs, first_gain.astype(jnp.float32), first_shift.astype(jnp.float32)
    )
    normed_low = normed_one.astype(jnp.bfloat16)
    projected = jnp.dot(normed_low, full_qkv, preferred_element_type=jnp.float32)
    queries = (projected[:, :model_width] + query_shift.astype(jnp.float32)).astype(jnp.bfloat16)
    key_rows = projected[:, model_width : 2 * model_width].astype(jnp.bfloat16)
    value_rows = (projected[:, 2 * model_width :] + value_shift.astype(jnp.float32)).astype(
        jnp.bfloat16
    )
    both_all = lax.all_gather(
        jnp.stack([key_rows, value_rows]).reshape(2, sequences, local_len, model_width),
        comm.group,
        axis=2,
        tiled=True,
    )
    key_all, value_all = both_all[0], both_all[1]
    full_len = key_all.shape[1]
    key_block = min(512, full_len)
    key_turns = full_len // key_block
    query_heads = queries.reshape(sequences, local_len, HEADS, HEAD_DIM)
    row_index = device_index * local_len + jnp.arange(local_len, dtype=jnp.int32)
    block_range = jnp.arange(key_block, dtype=jnp.int32)

    def key_slices(offset):
        key_heads = lax.dynamic_slice_in_dim(key_all, offset, key_block, 1).reshape(
            sequences, key_block, HEADS, HEAD_DIM
        )
        value_heads = lax.dynamic_slice_in_dim(value_all, offset, key_block, 1).reshape(
            sequences, key_block, HEADS, HEAD_DIM
        )
        return (key_heads, value_heads)

    def forward_step(block_index, running):
        highest, row_total, summed = running
        offset = block_index * key_block
        key_heads, value_heads = key_slices(offset)
        scores = masked_scores(query_heads, key_heads, row_index, offset + block_range, factor)
        new_high = jnp.maximum(highest, jnp.max(scores, axis=-1))
        fading = jnp.exp(highest - new_high)
        weights = jnp.exp(scores - new_high[..., None])
        row_total = row_total * fading + jnp.sum(weights, axis=-1)
        summed = summed * fading[..., None] + jnp.einsum(
            "shqk,skhe->shqe",
            weights.astype(jnp.bfloat16),
            value_heads,
            preferred_element_type=jnp.float32,
        )
        return (new_high, row_total, summed)

    start_state = (
        jnp.full((sequences, HEADS, local_len), MASKED, jnp.float32),
        jnp.zeros((sequences, HEADS, local_len), jnp.float32),
        jnp.zeros((sequences, HEADS, local_len, HEAD_DIM), jnp.float32),
    )
    highest, row_total, summed = lax.fori_loop(0, key_turns, forward_step, start_state)
    log_total = highest + jnp.log(row_total)
    attended = jnp.transpose(summed / row_total[..., None], (0, 2, 1, 3))
    attended_low = attended.reshape(row_count, model_width).astype(jnp.bfloat16)
    middle = (
        inputs
        + jnp.dot(attended_low, full_out, preferred_element_type=jnp.float32)
        + out_shift.astype(jnp.float32)
    )
    scaled_two, inverse_two, normed_two = norm_rows(
        middle, second_gain.astype(jnp.float32), second_shift.astype(jnp.float32)
    )
    second_low = normed_two.astype(jnp.bfloat16)
    pre_act = jnp.dot(second_low, full_up, preferred_element_type=jnp.float32) + up_shift.astype(
        jnp.float32
    )
    hidden_full, gelu_pull = jax.vjp(gelu_exact, pre_act)
    hidden = hidden_full.astype(jnp.bfloat16)
    result = (
        middle
        + jnp.dot(hidden, full_down, preferred_element_type=jnp.float32)
        + down_shift.astype(jnp.float32)
    )
    block_out = result.astype(jnp.bfloat16).reshape(sequences, local_len, model_width)
    back_gain_one, back_qkv, back_out = (first_gain, full_qkv, full_out)
    back_gain_two, back_up, back_down = (second_gain, full_up, full_down)
    upstream = out_grad.reshape(row_count, model_width)
    upstream_full = upstream.astype(jnp.float32)
    grad_down = comm.reduce(
        jnp.einsum("rf,rd->fd", hidden, upstream, preferred_element_type=jnp.float32).astype(
            jnp.bfloat16
        )
    )
    grad_down_shift = jnp.sum(upstream_full, axis=0)
    hidden_grad = jnp.einsum("rd,fd->rf", upstream, back_down, preferred_element_type=jnp.float32)
    pre_grad = gelu_pull(hidden_grad)[0].astype(jnp.bfloat16)
    grad_up = comm.reduce(
        jnp.einsum("rd,rf->df", second_low, pre_grad, preferred_element_type=jnp.float32).astype(
            jnp.bfloat16
        )
    )
    grad_up_shift = jnp.sum(pre_grad.astype(jnp.float32), axis=0)
    second_grad = jnp.einsum("rf,df->rd", pre_grad, back_up, preferred_element_type=jnp.float32)
    middle_norm_grad, grad_second_gain, grad_second_shift = norm_back(
        second_grad, scaled_two, inverse_two, back_gain_two.astype(jnp.float32)
    )
    middle_grad = upstream_full + middle_norm_grad
    middle_low = middle_grad.astype(jnp.bfloat16)
    grad_out = comm.reduce(
        jnp.einsum("re,rd->ed", attended_low, middle_low, preferred_element_type=jnp.float32).astype(
            jnp.bfloat16
        )
    )
    grad_out_shift = jnp.sum(middle_low.astype(jnp.float32), axis=0)
    attended_grad = jnp.einsum(
        "rd,ed->re", middle_low, back_out, preferred_element_type=jnp.float32
    ).astype(jnp.bfloat16)
    grad_heads = attended_grad.reshape(sequences, local_len, HEADS, HEAD_DIM)
    delta_rows = jnp.transpose(
        jnp.sum(grad_heads.astype(jnp.float32) * attended, axis=-1), (0, 2, 1)
    )
    query_start = jnp.zeros((sequences, local_len, HEADS, HEAD_DIM), jnp.float32)

    def backward_step(block_index, running):
        query_grad, key_grads, value_grads = running
        offset = block_index * key_block
        key_heads, value_heads = key_slices(offset)
        probs_low, score_grads = pair_terms(
            query_heads,
            grad_heads,
            key_heads,
            value_heads,
            row_index,
            offset + block_range,
            log_total,
            delta_rows,
            factor,
        )
        query_grad = (
            query_grad
            + jnp.einsum(
                "shqk,skhe->sqhe", score_grads, key_heads, preferred_element_type=jnp.float32
            )
            * factor
        )
        key_part = (
            jnp.einsum(
                "shqk,sqhe->skhe", score_grads, query_heads, preferred_element_type=jnp.float32
            )
            * factor
        )
        value_part = jnp.einsum(
            "shqk,sqhe->skhe", probs_low, grad_heads, preferred_element_type=jnp.float32
        )
        key_grads = lax.dynamic_update_slice_in_dim(
            key_grads, key_part.reshape(sequences, key_block, model_width), offset, 1
        )
        value_grads = lax.dynamic_update_slice_in_dim(
            value_grads, value_part.reshape(sequences, key_block, model_width), offset, 1
        )
        return (query_grad, key_grads, value_grads)

    start_back = (
        query_start,
        jnp.zeros((sequences, full_len, model_width), jnp.float32),
        jnp.zeros((sequences, full_len, model_width), jnp.float32),
    )
    query_grad, key_grads, value_grads = lax.fori_loop(0, key_turns, backward_step, start_back)
    query_low = query_grad.reshape(row_count, model_width).astype(jnp.bfloat16)
    own_both = comm.scatter_tokens(
        jnp.concatenate([key_grads, value_grads], axis=0).astype(jnp.bfloat16)
    ).reshape(2, row_count, model_width)
    qkv_grad = jnp.concatenate([query_low, own_both[0], own_both[1]], axis=1)
    early = model_width // 128 * 128
    grad_qkv = jnp.concatenate(
        [
            comm.reduce(
                jnp.einsum(
                    "rd,rc->dc", normed_low, part, preferred_element_type=jnp.float32
                ).astype(jnp.bfloat16)
            )
            for part in (query_low[:, :early], qkv_grad[:, early:])
        ],
        axis=1,
    )
    grad_query_shift = jnp.sum(qkv_grad[:, :model_width].astype(jnp.float32), axis=0)
    grad_value_shift = jnp.sum(qkv_grad[:, 2 * model_width :].astype(jnp.float32), axis=0)
    first_grad = jnp.einsum("rc,dc->rd", qkv_grad, back_qkv, preferred_element_type=jnp.float32)
    input_norm_grad, grad_first_gain, grad_first_shift = norm_back(
        first_grad, scaled_one, inverse_one, back_gain_one.astype(jnp.float32)
    )
    input_grad = (middle_grad + input_norm_grad).reshape(sequences, local_len, model_width)
    small = (
        grad_first_gain,
        grad_first_shift,
        grad_query_shift,
        grad_value_shift,
        grad_out_shift,
        grad_second_gain,
        grad_second_shift,
        grad_down_shift,
        grad_up_shift,
    )
    packed = jnp.concatenate([member.reshape(members, -1) for member in small], axis=1)
    summed_small = comm.reduce_small(packed)
    totals, position = [], 0
    for member in small:
        totals.append(summed_small[position : position + member.size // members])
        position = position + member.size // members
    return (
        block_out,
        input_grad,
        totals[0],
        totals[1],
        grad_qkv,
        totals[2],
        totals[3],
        grad_out,
        totals[4],
        totals[5],
        totals[6],
        grad_up,
        totals[8],
        grad_down,
        totals[7],
    )


def solution(mesh):
    comm, whole = AxisComm(), mesh
    if dict(mesh.shape) == {"replica": 8, "fsdp": 4}:
        comm = TorusComm()
        whole = jax.sharding.Mesh(mesh.devices.reshape(4, 2, 2, 2), ("z", "y", "x", "core"))
    sets, group = comm.sets, comm.group
    tokens, rows, vector = P(sets, group, None), P(group, None), P(group)
    placed = (
        tokens,
        vector,
        vector,
        rows,
        vector,
        vector,
        rows,
        vector,
        vector,
        vector,
        rows,
        vector,
        rows,
        vector,
        tokens,
    )
    return jax.shard_map(
        functools.partial(shards, comm),
        mesh=whole,
        in_specs=placed,
        out_specs=(
            tokens,
            tokens,
            vector,
            vector,
            rows,
            vector,
            vector,
            rows,
            vector,
            vector,
            vector,
            rows,
            vector,
            rows,
            vector,
        ),
        check_vma=False,
    )
```

```python
import functools
import math

import jax
import jax.numpy as jnp
from jax import lax
from jax.experimental.layout import Layout, with_layout_constraint
from jax.sharding import PartitionSpec as P

HEADS = 17
HEAD_DIM = 64


EPSILON = 1e-05
MASKED = -1e30
SWAP = ((0, 1), (1, 0))
NEAR = ((0, 1), (1, 0), (2, 3), (3, 2))
FAR = ((0, 2), (2, 0), (1, 3), (3, 1))


def norm_rows(values, gain, shift):
    center = values - jnp.mean(values, axis=-1, keepdims=True)
    inverse = lax.rsqrt(jnp.mean(center * center, axis=-1, keepdims=True) + EPSILON)
    scaled = center * inverse
    return (scaled, inverse, scaled * gain + shift)


def norm_back(upstream, scaled, inverse, gain):
    weighted = upstream * gain
    inner = (
        weighted
        - jnp.mean(weighted, axis=-1, keepdims=True)
        - scaled * jnp.mean(weighted * scaled, axis=-1, keepdims=True)
    )
    return (inverse * inner, jnp.sum(upstream * scaled, axis=0), jnp.sum(upstream, axis=0))


def gelu_exact(values):
    return 0.5 * values * (1.0 + jax.scipy.special.erf(values * (1.0 / math.sqrt(2.0))))


def masked_scores(row_heads, key_heads, row_index, key_index, factor):
    raw_scores = jnp.einsum(
        "sqhe,skhe->shqk", row_heads, key_heads, preferred_element_type=jnp.float32
    )
    allowed = key_index[None, :] <= row_index[:, None]
    return jnp.where(allowed[None, None], raw_scores * factor, MASKED)


def pair_terms(
    row_heads,
    grad_heads,
    key_heads,
    value_heads,
    row_index,
    key_index,
    log_total,
    delta_rows,
    factor,
):
    scores = masked_scores(row_heads, key_heads, row_index, key_index, factor)
    probs_full = jnp.exp(scores - log_total[..., None])
    prob_grads = jnp.einsum(
        "sqhe,skhe->shqk", grad_heads, value_heads, preferred_element_type=jnp.float32
    )
    score_grads = (probs_full * (prob_grads - delta_rows[..., None])).astype(jnp.bfloat16)
    return (probs_full.astype(jnp.bfloat16), score_grads)


class AxisComm:
    group = "fsdp"
    sets = "replica"

    def gather_all(self, vector, shards):
        every = lax.all_gather(vector, "fsdp", axis=0)
        return every, [lax.all_gather(shard, "fsdp", axis=0, tiled=True) for shard in shards]

    def near_sum(self, local):
        return local

    def group_sum(self, local):
        return lax.psum_scatter(local, "fsdp", scatter_dimension=0, tiled=True)

    def set_sum(self, owned):
        return lax.psum(owned, "replica")

    def reduce_small(self, packed):
        total = lax.psum(packed, ("replica", "fsdp"))
        return lax.dynamic_index_in_dim(total, lax.axis_index("fsdp"), 0, keepdims=False)


def split_half(rows):
    size = -(-rows // 16) * 8
    return (size, rows - size)


def halve(array, name, pairs, place):
    size, second = split_half(array.shape[0])
    keep = lax.dynamic_slice_in_dim(array, place * second, size, 0)
    send = lax.dynamic_slice_in_dim(array, (1 - place) * second, size, 0)
    got = lax.ppermute(send, name, pairs)
    return (keep.astype(jnp.float32) + got.astype(jnp.float32)).astype(array.dtype)


def join(array, name, pairs, place, rows):
    _, second = split_half(rows)
    got = lax.ppermute(array, name, pairs)
    low = jnp.where(place == 0, array, got)
    high = jnp.where(place == 0, got, array)
    return jnp.concatenate([low[:second], high], axis=0)


def add_low(one, two):
    return (one.astype(jnp.float32) + two.astype(jnp.float32)).astype(one.dtype)


class TorusComm:
    group = ("x", "core")
    sets = ("z", "y")

    def finish_gather(self, shard, beside, far):
        x, core = lax.axis_index("x"), lax.axis_index("core")
        far_beside = lax.ppermute(far, "core", SWAP)
        near_first = jnp.where(core == 0, shard, beside)
        near_second = jnp.where(core == 0, beside, shard)
        far_first = jnp.where(core == 0, far, far_beside)
        far_second = jnp.where(core == 0, far_beside, far)
        return jnp.concatenate(
            [
                jnp.where(x == 0, near_first, far_first),
                jnp.where(x == 0, near_second, far_second),
                jnp.where(x == 0, far_first, near_first),
                jnp.where(x == 0, far_second, near_second),
            ],
            axis=0,
        )

    def gather_all(self, vector, shards):
        y = lax.axis_index("y")
        row = vector.reshape(1, -1)
        every = self.finish_gather(
            row, lax.ppermute(row, "core", SWAP), lax.ppermute(row, "x", SWAP)
        )
        whole, order = [], every
        for shard in shards:
            half = shard.shape[0] // 2
            beside = lax.ppermute(shard, "core", SWAP)
            piece = lax.dynamic_slice_in_dim(shard, y * half, half, 0)
            piece, order = lax.optimization_barrier((piece, order))
            got = lax.ppermute(piece, "x", SWAP)
            order = got
            other = lax.ppermute(got, "y", SWAP)
            far = jnp.concatenate(
                [jnp.where(y == 0, got, other), jnp.where(y == 0, other, got)], axis=0
            )
            whole.append(self.finish_gather(shard, beside, far))
        return every, whole

    def near_sum(self, local):
        x, core = lax.axis_index("x"), lax.axis_index("core")
        rows = local.shape[0] // 4

        def block(chip, side):
            return lax.dynamic_slice_in_dim(local, (2 * chip + side) * rows, rows, 0)

        return tuple(
            add_low(block(chip, core), lax.ppermute(block(chip, 1 - core), "core", SWAP))
            for chip in (1 - x, x)
        )

    def group_sum(self, sums):
        far, near = sums
        return add_low(near, lax.ppermute(far, "x", SWAP))

    def set_sum(self, own):
        y, z = lax.axis_index("y"), lax.axis_index("z")
        steps = (("y", SWAP, y), ("z", NEAR, lax.rem(z, 2)), ("z", FAR, lax.div(z, 2)))
        sizes = []
        for name, pairs, place in steps:
            sizes.append(own.shape[0])
            own = halve(own, name, pairs, place)
        for (name, pairs, place), size in zip(steps[::-1], sizes[::-1]):
            own = join(own, name, pairs, place, size)
        return own

    def reduce_small(self, packed):
        for name, pairs in (
            ("core", SWAP),
            ("x", SWAP),
            ("y", SWAP),
            ("z", NEAR),
            ("z", FAR),
        ):
            packed = packed + lax.ppermute(packed, name, pairs)
        place = lax.axis_index("x") * 2 + lax.axis_index("core")
        return lax.dynamic_index_in_dim(packed, place, 0, keepdims=False)


def weight_grad(rows, columns):
    product = lax.dot_general(
        rows, columns, (((0,), (0,)), ((), ())), preferred_element_type=jnp.float32
    ).astype(jnp.bfloat16)
    return with_layout_constraint(product, Layout(major_to_minor=(0, 1)))


def shards(
    comm,
    tokens_in,
    norm1_gain,
    norm1_bias,
    qkv_weight,
    query_bias,
    value_bias,
    out_weight,
    out_bias,
    norm2_gain,
    norm2_bias,
    up_weight,
    up_bias,
    down_weight,
    down_bias,
    out_grad,
):
    vectors = (
        norm1_gain,
        norm1_bias,
        query_bias,
        value_bias,
        out_bias,
        norm2_gain,
        norm2_bias,
        down_bias,
        up_bias,
    )
    members = lax.axis_size(comm.group)
    every, (full_qkv, full_out, full_up, full_down) = comm.gather_all(
        jnp.concatenate(vectors), (qkv_weight, out_weight, up_weight, down_weight)
    )
    pieces, position = [], 0
    for member in vectors:
        pieces.append(every[:, position : position + member.size].reshape(-1))
        position = position + member.size
    (
        first_gain,
        first_shift,
        query_shift,
        value_shift,
        out_shift,
        second_gain,
        second_shift,
        down_shift,
        up_shift,
    ) = pieces
    sequences, local_len, model_width = tokens_in.shape
    row_count = sequences * local_len
    device_index = lax.axis_index(comm.group)
    factor = 1.0 / math.sqrt(HEAD_DIM)
    inputs = tokens_in.astype(jnp.float32).reshape(row_count, model_width)
    scaled_one, inverse_one, normed_one = norm_rows(
        inputs, first_gain.astype(jnp.float32), first_shift.astype(jnp.float32)
    )
    normed_low = normed_one.astype(jnp.bfloat16)
    projected = jnp.dot(normed_low, full_qkv, preferred_element_type=jnp.float32)
    queries = (projected[:, :model_width] + query_shift.astype(jnp.float32)).astype(jnp.bfloat16)
    key_rows = projected[:, model_width : 2 * model_width].astype(jnp.bfloat16)
    value_rows = (projected[:, 2 * model_width :] + value_shift.astype(jnp.float32)).astype(
        jnp.bfloat16
    )
    both_all = lax.all_gather(
        jnp.stack([key_rows, value_rows]).reshape(2, sequences, local_len, model_width),
        comm.group,
        axis=2,
        tiled=True,
    )
    key_all, value_all = both_all[0], both_all[1]
    full_len = key_all.shape[1]
    key_block = min(1024, full_len)
    key_turns = full_len // key_block
    query_heads = queries.reshape(sequences, local_len, HEADS, HEAD_DIM)
    row_index = device_index * local_len + jnp.arange(local_len, dtype=jnp.int32)
    block_range = jnp.arange(key_block, dtype=jnp.int32)

    def key_slices(offset):
        key_heads = lax.dynamic_slice_in_dim(key_all, offset, key_block, 1).reshape(
            sequences, key_block, HEADS, HEAD_DIM
        )
        value_heads = lax.dynamic_slice_in_dim(value_all, offset, key_block, 1).reshape(
            sequences, key_block, HEADS, HEAD_DIM
        )
        return (key_heads, value_heads)

    def forward_step(block_index, running):
        highest, row_total, summed = running
        offset = block_index * key_block
        key_heads, value_heads = key_slices(offset)
        scores = masked_scores(query_heads, key_heads, row_index, offset + block_range, factor)
        new_high = jnp.maximum(highest, jnp.max(scores, axis=-1))
        fading = jnp.exp(highest - new_high)
        weights = jnp.exp(scores - new_high[..., None])
        row_total = row_total * fading + jnp.sum(weights, axis=-1)
        summed = summed * fading[..., None] + jnp.einsum(
            "shqk,skhe->shqe",
            weights.astype(jnp.bfloat16),
            value_heads,
            preferred_element_type=jnp.float32,
        )
        return (new_high, row_total, summed)

    start_state = (
        jnp.full((sequences, HEADS, local_len), MASKED, jnp.float32),
        jnp.zeros((sequences, HEADS, local_len), jnp.float32),
        jnp.zeros((sequences, HEADS, local_len, HEAD_DIM), jnp.float32),
    )
    highest, row_total, summed = lax.fori_loop(0, key_turns, forward_step, start_state)
    log_total = highest + jnp.log(row_total)
    attended = jnp.transpose(summed / row_total[..., None], (0, 2, 1, 3))
    attended_low = attended.reshape(row_count, model_width).astype(jnp.bfloat16)
    middle = (
        inputs
        + jnp.dot(attended_low, full_out, preferred_element_type=jnp.float32)
        + out_shift.astype(jnp.float32)
    )
    scaled_two, inverse_two, normed_two = norm_rows(
        middle, second_gain.astype(jnp.float32), second_shift.astype(jnp.float32)
    )
    second_low = normed_two.astype(jnp.bfloat16)
    pre_act = jnp.dot(second_low, full_up, preferred_element_type=jnp.float32) + up_shift.astype(
        jnp.float32
    )
    hidden_full, gelu_pull = jax.vjp(gelu_exact, pre_act)
    hidden = hidden_full.astype(jnp.bfloat16)
    result = (
        middle
        + jnp.dot(hidden, full_down, preferred_element_type=jnp.float32)
        + down_shift.astype(jnp.float32)
    )
    block_out = result.astype(jnp.bfloat16).reshape(sequences, local_len, model_width)
    back_gain_one, back_qkv, back_out = (first_gain, full_qkv, full_out)
    back_gain_two, back_up, back_down = (second_gain, full_up, full_down)
    upstream = out_grad.reshape(row_count, model_width)
    upstream_full = upstream.astype(jnp.float32)
    down_near = comm.near_sum(weight_grad(hidden, upstream))
    grad_down_shift = jnp.sum(upstream_full, axis=0)
    hidden_grad = jnp.einsum("rd,fd->rf", upstream, back_down, preferred_element_type=jnp.float32)
    hidden_grad, down_near = lax.optimization_barrier((hidden_grad, down_near))
    pre_grad = gelu_pull(hidden_grad)[0].astype(jnp.bfloat16)
    up_near = comm.near_sum(weight_grad(second_low, pre_grad))
    grad_up_shift = jnp.sum(pre_grad.astype(jnp.float32), axis=0)
    second_grad = jnp.einsum("rf,df->rd", pre_grad, back_up, preferred_element_type=jnp.float32)
    middle_norm_grad, grad_second_gain, grad_second_shift = norm_back(
        second_grad, scaled_two, inverse_two, back_gain_two.astype(jnp.float32)
    )
    middle_grad = upstream_full + middle_norm_grad
    middle_low = middle_grad.astype(jnp.bfloat16)
    out_near = comm.near_sum(weight_grad(attended_low, middle_low))
    grad_out_shift = jnp.sum(middle_low.astype(jnp.float32), axis=0)
    attended_grad = jnp.einsum(
        "rd,ed->re", middle_low, back_out, preferred_element_type=jnp.float32
    ).astype(jnp.bfloat16)
    attended_grad, up_near, out_near = lax.optimization_barrier(
        (attended_grad, up_near, out_near)
    )
    down_owned = comm.group_sum(down_near)
    grad_heads = attended_grad.reshape(sequences, local_len, HEADS, HEAD_DIM)
    delta_rows = jnp.transpose(
        jnp.sum(grad_heads.astype(jnp.float32) * attended, axis=-1), (0, 2, 1)
    )
    query_start = jnp.zeros((sequences, local_len, HEADS, HEAD_DIM), jnp.float32)

    def backward_step(block_index, running):
        query_grad, key_grads, value_grads = running
        offset = block_index * key_block
        key_heads, value_heads = key_slices(offset)
        probs_low, score_grads = pair_terms(
            query_heads,
            grad_heads,
            key_heads,
            value_heads,
            row_index,
            offset + block_range,
            log_total,
            delta_rows,
            factor,
        )
        query_grad = (
            query_grad
            + jnp.einsum(
                "shqk,skhe->sqhe", score_grads, key_heads, preferred_element_type=jnp.float32
            )
            * factor
        )
        key_part = (
            jnp.einsum(
                "shqk,sqhe->skhe", score_grads, query_heads, preferred_element_type=jnp.float32
            )
            * factor
        )
        value_part = jnp.einsum(
            "shqk,sqhe->skhe", probs_low, grad_heads, preferred_element_type=jnp.float32
        )
        key_grads = lax.dynamic_update_slice_in_dim(
            key_grads, key_part.reshape(sequences, key_block, model_width), offset, 1
        )
        value_grads = lax.dynamic_update_slice_in_dim(
            value_grads, value_part.reshape(sequences, key_block, model_width), offset, 1
        )
        return (query_grad, key_grads, value_grads)

    start_back = (
        query_start,
        jnp.zeros((sequences, full_len, model_width), jnp.float32),
        jnp.zeros((sequences, full_len, model_width), jnp.float32),
    )
    query_grad, key_grads, value_grads = lax.fori_loop(0, key_turns, backward_step, start_back)
    query_low = query_grad.reshape(row_count, model_width).astype(jnp.bfloat16)
    both_grads = jnp.concatenate(
        [
            jnp.moveaxis(member.astype(jnp.bfloat16), 0, 1).reshape(full_len, -1)
            for member in (key_grads, value_grads)
        ],
        axis=1,
    )
    both_near = comm.near_sum(both_grads)
    early = model_width // 128 * 128
    early_near = comm.near_sum(weight_grad(normed_low, query_low[:, :early]))
    both_near, early_near, down_owned = lax.optimization_barrier(
        (both_near, early_near, down_owned)
    )
    own_both = comm.group_sum(both_near)
    up_owned = comm.group_sum(up_near)
    own_both, up_owned = lax.optimization_barrier((own_both, up_owned))
    key_low, value_low = (
        jnp.moveaxis(member.reshape(local_len, sequences, model_width), 0, 1).reshape(
            row_count, model_width
        )
        for member in jnp.split(own_both, 2, axis=1)
    )
    qkv_grad = jnp.concatenate([query_low, key_low, value_low], axis=1)
    late_near = comm.near_sum(weight_grad(normed_low, qkv_grad[:, early:]))
    grad_down, grad_up, grad_out = (
        comm.set_sum(owned).astype(jnp.float32)
        for owned in (down_owned, up_owned, comm.group_sum(out_near))
    )
    grad_qkv = jnp.concatenate(
        [
            comm.set_sum(comm.group_sum(near)).astype(jnp.float32)
            for near in (early_near, late_near)
        ],
        axis=1,
    )
    grad_query_shift = jnp.sum(qkv_grad[:, :model_width].astype(jnp.float32), axis=0)
    grad_value_shift = jnp.sum(qkv_grad[:, 2 * model_width :].astype(jnp.float32), axis=0)
    first_grad = jnp.einsum("rc,dc->rd", qkv_grad, back_qkv, preferred_element_type=jnp.float32)
    input_norm_grad, grad_first_gain, grad_first_shift = norm_back(
        first_grad, scaled_one, inverse_one, back_gain_one.astype(jnp.float32)
    )
    input_grad = (middle_grad + input_norm_grad).reshape(sequences, local_len, model_width)
    small = (
        grad_first_gain,
        grad_first_shift,
        grad_query_shift,
        grad_value_shift,
        grad_out_shift,
        grad_second_gain,
        grad_second_shift,
        grad_down_shift,
        grad_up_shift,
    )
    packed = jnp.concatenate([member.reshape(members, -1) for member in small], axis=1)
    summed_small = comm.reduce_small(packed)
    totals, position = [], 0
    for member in small:
        totals.append(summed_small[position : position + member.size // members])
        position = position + member.size // members
    return (
        block_out,
        input_grad,
        totals[0],
        totals[1],
        grad_qkv,
        totals[2],
        totals[3],
        grad_out,
        totals[4],
        totals[5],
        totals[6],
        grad_up,
        totals[8],
        grad_down,
        totals[7],
    )


def solution(mesh):
    comm, whole = AxisComm(), mesh
    if dict(mesh.shape) == {"replica": 8, "fsdp": 4}:
        comm = TorusComm()
        whole = jax.sharding.Mesh(mesh.devices.reshape(4, 2, 2, 2), ("z", "y", "x", "core"))
    sets, group = comm.sets, comm.group
    tokens, rows, vector = P(sets, group, None), P(group, None), P(group)
    placed = (
        tokens,
        vector,
        vector,
        rows,
        vector,
        vector,
        rows,
        vector,
        vector,
        vector,
        rows,
        vector,
        rows,
        vector,
        tokens,
    )
    return jax.shard_map(
        functools.partial(shards, comm),
        mesh=whole,
        in_specs=placed,
        out_specs=(
            tokens,
            tokens,
            vector,
            vector,
            rows,
            vector,
            vector,
            rows,
            vector,
            vector,
            vector,
            rows,
            vector,
            rows,
            vector,
        ),
        check_vma=False,
    )
```

```python
import functools
import math

import jax
import jax.numpy as jnp
from jax import lax
from jax.experimental.layout import Layout, with_layout_constraint
from jax.sharding import PartitionSpec as P

HEADS = 17
HEAD_DIM = 64


EPSILON = 1e-05
MASKED = -1e30
SWAP = ((0, 1), (1, 0))
NEAR = ((0, 1), (1, 0), (2, 3), (3, 2))
FAR = ((0, 2), (2, 0), (1, 3), (3, 1))


def norm_rows(values, gain, shift):
    center = values - jnp.mean(values, axis=-1, keepdims=True)
    inverse = lax.rsqrt(jnp.mean(center * center, axis=-1, keepdims=True) + EPSILON)
    scaled = center * inverse
    return (scaled, inverse, scaled * gain + shift)


def norm_back(upstream, scaled, inverse, gain):
    weighted = upstream * gain
    inner = (
        weighted
        - jnp.mean(weighted, axis=-1, keepdims=True)
        - scaled * jnp.mean(weighted * scaled, axis=-1, keepdims=True)
    )
    return (inverse * inner, jnp.sum(upstream * scaled, axis=0), jnp.sum(upstream, axis=0))


def gelu_exact(values):
    return 0.5 * values * (1.0 + jax.scipy.special.erf(values * (1.0 / math.sqrt(2.0))))


def masked_scores(row_heads, key_heads, row_index, key_index, factor):
    raw_scores = jnp.einsum(
        "sqhe,skhe->shqk", row_heads, key_heads, preferred_element_type=jnp.float32
    )
    allowed = key_index[None, :] <= row_index[:, None]
    return jnp.where(allowed[None, None], raw_scores * factor, MASKED)


def pair_terms(
    row_heads,
    grad_heads,
    key_heads,
    value_heads,
    row_index,
    key_index,
    log_total,
    delta_rows,
    factor,
):
    scores = masked_scores(row_heads, key_heads, row_index, key_index, factor)
    probs_full = jnp.exp(scores - log_total[..., None])
    prob_grads = jnp.einsum(
        "sqhe,skhe->shqk", grad_heads, value_heads, preferred_element_type=jnp.float32
    )
    score_grads = (probs_full * (prob_grads - delta_rows[..., None])).astype(jnp.bfloat16)
    return (probs_full.astype(jnp.bfloat16), score_grads)


class AxisComm:
    group = "fsdp"
    sets = "replica"

    def gather_vectors(self, vector):
        return lax.all_gather(vector, "fsdp", axis=0)

    def gather(self, shard, order):
        return lax.all_gather(shard, "fsdp", axis=0, tiled=True), order

    def near_sum(self, local):
        return local

    def group_sum(self, local):
        return lax.psum_scatter(local, "fsdp", scatter_dimension=0, tiled=True)

    def set_share(self, owned):
        return lax.psum(owned, "replica")

    def set_join(self, share, rows):
        return share

    def reduce_small(self, packed):
        total = lax.psum(packed, ("replica", "fsdp"))
        return lax.dynamic_index_in_dim(total, lax.axis_index("fsdp"), 0, keepdims=False)


def split_half(rows):
    size = -(-rows // 16) * 8
    return (size, rows - size)


def halve(array, name, pairs, place):
    size, second = split_half(array.shape[0])
    keep = lax.dynamic_slice_in_dim(array, place * second, size, 0)
    send = lax.dynamic_slice_in_dim(array, (1 - place) * second, size, 0)
    got = lax.ppermute(send, name, pairs)
    return (keep.astype(jnp.float32) + got.astype(jnp.float32)).astype(array.dtype)


def join(array, name, pairs, place, rows):
    _, second = split_half(rows)
    got = lax.ppermute(array, name, pairs)
    low = jnp.where(place == 0, array, got)
    high = jnp.where(place == 0, got, array)
    return jnp.concatenate([low[:second], high], axis=0)


def add_low(one, two):
    return (one.astype(jnp.float32) + two.astype(jnp.float32)).astype(one.dtype)


class TorusComm:
    group = ("x", "core")
    sets = ("z", "y")

    def finish_gather(self, shard, beside, far):
        x, core = lax.axis_index("x"), lax.axis_index("core")
        far_beside = lax.ppermute(far, "core", SWAP)
        near_first = jnp.where(core == 0, shard, beside)
        near_second = jnp.where(core == 0, beside, shard)
        far_first = jnp.where(core == 0, far, far_beside)
        far_second = jnp.where(core == 0, far_beside, far)
        return jnp.concatenate(
            [
                jnp.where(x == 0, near_first, far_first),
                jnp.where(x == 0, near_second, far_second),
                jnp.where(x == 0, far_first, near_first),
                jnp.where(x == 0, far_second, near_second),
            ],
            axis=0,
        )

    def gather_vectors(self, vector):
        row = vector.reshape(1, -1)
        return self.finish_gather(
            row, lax.ppermute(row, "core", SWAP), lax.ppermute(row, "x", SWAP)
        )

    def gather(self, shard, order):
        y = lax.axis_index("y")
        half = shard.shape[0] // 2
        beside = lax.ppermute(shard, "core", SWAP)
        piece = lax.dynamic_slice_in_dim(shard, y * half, half, 0)
        piece, _ = lax.optimization_barrier((piece, order))
        got = lax.ppermute(piece, "x", SWAP)
        other = lax.ppermute(got, "y", SWAP)
        far = jnp.concatenate(
            [jnp.where(y == 0, got, other), jnp.where(y == 0, other, got)], axis=0
        )
        return self.finish_gather(shard, beside, far), got

    def near_sum(self, local):
        x, core = lax.axis_index("x"), lax.axis_index("core")
        rows = local.shape[0] // 4

        def block(chip, side):
            return lax.dynamic_slice_in_dim(local, (2 * chip + side) * rows, rows, 0)

        return tuple(
            add_low(block(chip, core), lax.ppermute(block(chip, 1 - core), "core", SWAP))
            for chip in (1 - x, x)
        )

    def group_sum(self, sums):
        far, near = sums
        return add_low(near, lax.ppermute(far, "x", SWAP))

    def set_steps(self):
        y, z = lax.axis_index("y"), lax.axis_index("z")
        return (("y", SWAP, y), ("z", NEAR, lax.rem(z, 2)), ("z", FAR, lax.div(z, 2)))

    def set_share(self, own):
        for name, pairs, place in self.set_steps():
            own = halve(own, name, pairs, place)
        return own

    def set_join(self, share, rows):
        sizes = [rows]
        for _ in range(2):
            sizes.append(split_half(sizes[-1])[0])
        for (name, pairs, place), size in zip(self.set_steps()[::-1], sizes[::-1]):
            share = join(share, name, pairs, place, size)
        return share

    def reduce_small(self, packed):
        for name, pairs in (
            ("core", SWAP),
            ("x", SWAP),
            ("y", SWAP),
            ("z", NEAR),
            ("z", FAR),
        ):
            packed = packed + lax.ppermute(packed, name, pairs)
        place = lax.axis_index("x") * 2 + lax.axis_index("core")
        return lax.dynamic_index_in_dim(packed, place, 0, keepdims=False)


def weight_grad(rows, columns):
    product = lax.dot_general(
        rows, columns, (((0,), (0,)), ((), ())), preferred_element_type=jnp.float32
    ).astype(jnp.bfloat16)
    return with_layout_constraint(product, Layout(major_to_minor=(0, 1)))


def shards(
    comm,
    tokens_in,
    norm1_gain,
    norm1_bias,
    qkv_weight,
    query_bias,
    value_bias,
    out_weight,
    out_bias,
    norm2_gain,
    norm2_bias,
    up_weight,
    up_bias,
    down_weight,
    down_bias,
    out_grad,
):
    vectors = (
        norm1_gain,
        norm1_bias,
        query_bias,
        value_bias,
        out_bias,
        norm2_gain,
        norm2_bias,
        down_bias,
        up_bias,
    )
    members = lax.axis_size(comm.group)
    every = comm.gather_vectors(jnp.concatenate(vectors))
    full_qkv, order = comm.gather(qkv_weight, every)
    full_out, _ = comm.gather(out_weight, order)
    full_up, _ = comm.gather(up_weight, order)
    pieces, position = [], 0
    for member in vectors:
        pieces.append(every[:, position : position + member.size].reshape(-1))
        position = position + member.size
    (
        first_gain,
        first_shift,
        query_shift,
        value_shift,
        out_shift,
        second_gain,
        second_shift,
        down_shift,
        up_shift,
    ) = pieces
    sequences, local_len, model_width = tokens_in.shape
    row_count = sequences * local_len
    device_index = lax.axis_index(comm.group)
    factor = 1.0 / math.sqrt(HEAD_DIM)
    inputs = tokens_in.astype(jnp.float32).reshape(row_count, model_width)
    scaled_one, inverse_one, normed_one = norm_rows(
        inputs, first_gain.astype(jnp.float32), first_shift.astype(jnp.float32)
    )
    normed_low = normed_one.astype(jnp.bfloat16)
    projected = jnp.dot(normed_low, full_qkv, preferred_element_type=jnp.float32)
    queries = (projected[:, :model_width] + query_shift.astype(jnp.float32)).astype(jnp.bfloat16)
    key_rows = projected[:, model_width : 2 * model_width].astype(jnp.bfloat16)
    value_rows = (projected[:, 2 * model_width :] + value_shift.astype(jnp.float32)).astype(
        jnp.bfloat16
    )
    both_all = lax.all_gather(
        jnp.stack([key_rows, value_rows]).reshape(2, sequences, local_len, model_width),
        comm.group,
        axis=2,
        tiled=True,
    )
    key_all, value_all = both_all[0], both_all[1]
    full_down, _ = comm.gather(down_weight, both_all)
    full_len = key_all.shape[1]
    key_block = min(1024, full_len)
    key_turns = full_len // key_block
    query_heads = queries.reshape(sequences, local_len, HEADS, HEAD_DIM)
    row_index = device_index * local_len + jnp.arange(local_len, dtype=jnp.int32)
    block_range = jnp.arange(key_block, dtype=jnp.int32)

    def key_slices(offset):
        key_heads = lax.dynamic_slice_in_dim(key_all, offset, key_block, 1).reshape(
            sequences, key_block, HEADS, HEAD_DIM
        )
        value_heads = lax.dynamic_slice_in_dim(value_all, offset, key_block, 1).reshape(
            sequences, key_block, HEADS, HEAD_DIM
        )
        return (key_heads, value_heads)

    def forward_step(block_index, running):
        highest, row_total, summed = running
        offset = block_index * key_block
        key_heads, value_heads = key_slices(offset)
        scores = masked_scores(query_heads, key_heads, row_index, offset + block_range, factor)
        new_high = jnp.maximum(highest, jnp.max(scores, axis=-1))
        fading = jnp.exp(highest - new_high)
        weights = jnp.exp(scores - new_high[..., None])
        row_total = row_total * fading + jnp.sum(weights, axis=-1)
        summed = summed * fading[..., None] + jnp.einsum(
            "shqk,skhe->shqe",
            weights.astype(jnp.bfloat16),
            value_heads,
            preferred_element_type=jnp.float32,
        )
        return (new_high, row_total, summed)

    start_state = (
        jnp.full((sequences, HEADS, local_len), MASKED, jnp.float32),
        jnp.zeros((sequences, HEADS, local_len), jnp.float32),
        jnp.zeros((sequences, HEADS, local_len, HEAD_DIM), jnp.float32),
    )
    highest, row_total, summed = lax.fori_loop(0, key_turns, forward_step, start_state)
    log_total = highest + jnp.log(row_total)
    attended = jnp.transpose(summed / row_total[..., None], (0, 2, 1, 3))
    attended_low = attended.reshape(row_count, model_width).astype(jnp.bfloat16)
    middle = (
        inputs
        + jnp.dot(attended_low, full_out, preferred_element_type=jnp.float32)
        + out_shift.astype(jnp.float32)
    )
    scaled_two, inverse_two, normed_two = norm_rows(
        middle, second_gain.astype(jnp.float32), second_shift.astype(jnp.float32)
    )
    second_low = normed_two.astype(jnp.bfloat16)
    pre_act = jnp.dot(second_low, full_up, preferred_element_type=jnp.float32) + up_shift.astype(
        jnp.float32
    )
    hidden_full, gelu_pull = jax.vjp(gelu_exact, pre_act)
    hidden = hidden_full.astype(jnp.bfloat16)
    result = (
        middle
        + jnp.dot(hidden, full_down, preferred_element_type=jnp.float32)
        + down_shift.astype(jnp.float32)
    )
    block_out = result.astype(jnp.bfloat16).reshape(sequences, local_len, model_width)
    back_gain_one, back_qkv, back_out = (first_gain, full_qkv, full_out)
    back_gain_two, back_up, back_down = (second_gain, full_up, full_down)
    upstream = out_grad.reshape(row_count, model_width)
    upstream_full = upstream.astype(jnp.float32)
    down_near = comm.near_sum(weight_grad(hidden, upstream))
    grad_down_shift = jnp.sum(upstream_full, axis=0)
    hidden_grad = jnp.einsum("rd,fd->rf", upstream, back_down, preferred_element_type=jnp.float32)
    hidden_grad, down_near = lax.optimization_barrier((hidden_grad, down_near))
    down_owned = comm.group_sum(down_near)
    pre_grad = gelu_pull(hidden_grad)[0].astype(jnp.bfloat16)
    up_near = comm.near_sum(weight_grad(second_low, pre_grad))
    grad_up_shift = jnp.sum(pre_grad.astype(jnp.float32), axis=0)
    second_grad = jnp.einsum("rf,df->rd", pre_grad, back_up, preferred_element_type=jnp.float32)
    middle_norm_grad, grad_second_gain, grad_second_shift = norm_back(
        second_grad, scaled_two, inverse_two, back_gain_two.astype(jnp.float32)
    )
    middle_grad = upstream_full + middle_norm_grad
    middle_low = middle_grad.astype(jnp.bfloat16)
    out_near = comm.near_sum(weight_grad(attended_low, middle_low))
    grad_out_shift = jnp.sum(middle_low.astype(jnp.float32), axis=0)
    attended_grad = jnp.einsum(
        "rd,ed->re", middle_low, back_out, preferred_element_type=jnp.float32
    ).astype(jnp.bfloat16)
    attended_grad, up_near, out_near = lax.optimization_barrier(
        (attended_grad, up_near, out_near)
    )
    up_owned = comm.group_sum(up_near)
    grad_heads = attended_grad.reshape(sequences, local_len, HEADS, HEAD_DIM)
    delta_rows = jnp.transpose(
        jnp.sum(grad_heads.astype(jnp.float32) * attended, axis=-1), (0, 2, 1)
    )
    query_start = jnp.zeros((sequences, local_len, HEADS, HEAD_DIM), jnp.float32)

    def backward_step(block_index, running):
        query_grad, key_grads, value_grads = running
        offset = block_index * key_block
        key_heads, value_heads = key_slices(offset)
        probs_low, score_grads = pair_terms(
            query_heads,
            grad_heads,
            key_heads,
            value_heads,
            row_index,
            offset + block_range,
            log_total,
            delta_rows,
            factor,
        )
        query_grad = (
            query_grad
            + jnp.einsum(
                "shqk,skhe->sqhe", score_grads, key_heads, preferred_element_type=jnp.float32
            )
            * factor
        )
        key_part = (
            jnp.einsum(
                "shqk,sqhe->skhe", score_grads, query_heads, preferred_element_type=jnp.float32
            )
            * factor
        )
        value_part = jnp.einsum(
            "shqk,sqhe->skhe", probs_low, grad_heads, preferred_element_type=jnp.float32
        )
        key_grads = lax.dynamic_update_slice_in_dim(
            key_grads, key_part.reshape(sequences, key_block, model_width), offset, 1
        )
        value_grads = lax.dynamic_update_slice_in_dim(
            value_grads, value_part.reshape(sequences, key_block, model_width), offset, 1
        )
        return (query_grad, key_grads, value_grads)

    start_back = (
        query_start,
        jnp.zeros((sequences, full_len, model_width), jnp.float32),
        jnp.zeros((sequences, full_len, model_width), jnp.float32),
    )
    query_grad, key_grads, value_grads = lax.fori_loop(0, key_turns, backward_step, start_back)
    query_grad, key_grads, value_grads, down_owned = lax.optimization_barrier(
        (query_grad, key_grads, value_grads, down_owned)
    )
    down_share = comm.set_share(down_owned)
    query_low = query_grad.reshape(row_count, model_width).astype(jnp.bfloat16)
    both_grads = jnp.concatenate(
        [
            jnp.moveaxis(member.astype(jnp.bfloat16), 0, 1).reshape(full_len, -1)
            for member in (key_grads, value_grads)
        ],
        axis=1,
    )
    both_near = comm.near_sum(both_grads)
    early = model_width // 128 * 128
    early_near = comm.near_sum(weight_grad(normed_low, query_low[:, :early]))
    both_near, early_near, up_owned, out_near = lax.optimization_barrier(
        (both_near, early_near, up_owned, out_near)
    )
    own_both = comm.group_sum(both_near)
    up_share = comm.set_share(up_owned)
    own_both, down_share, early_near, out_near = lax.optimization_barrier(
        (own_both, down_share, early_near, out_near)
    )
    out_owned = comm.group_sum(out_near)
    early_owned = comm.group_sum(early_near)
    key_low, value_low = (
        jnp.moveaxis(member.reshape(local_len, sequences, model_width), 0, 1).reshape(
            row_count, model_width
        )
        for member in jnp.split(own_both, 2, axis=1)
    )
    qkv_grad = jnp.concatenate([query_low, key_low, value_low], axis=1)
    late_near = comm.near_sum(weight_grad(normed_low, qkv_grad[:, early:]))
    late_near, up_share = lax.optimization_barrier((late_near, up_share))
    late_owned = comm.group_sum(late_near)
    out_share, early_share, late_share = (
        comm.set_share(owned) for owned in (out_owned, early_owned, late_owned)
    )
    down_sum, up_sum, out_sum, early_sum, late_sum = (
        comm.set_join(share, owner.shape[0]).astype(jnp.float32)
        for share, owner in (
            (down_share, down_weight),
            (up_share, up_weight),
            (out_share, out_weight),
            (early_share, qkv_weight),
            (late_share, qkv_weight),
        )
    )
    grad_down, grad_up, grad_out = down_sum, up_sum, out_sum
    grad_qkv = jnp.concatenate([early_sum, late_sum], axis=1)
    grad_query_shift = jnp.sum(qkv_grad[:, :model_width].astype(jnp.float32), axis=0)
    grad_value_shift = jnp.sum(qkv_grad[:, 2 * model_width :].astype(jnp.float32), axis=0)
    first_grad = jnp.einsum("rc,dc->rd", qkv_grad, back_qkv, preferred_element_type=jnp.float32)
    input_norm_grad, grad_first_gain, grad_first_shift = norm_back(
        first_grad, scaled_one, inverse_one, back_gain_one.astype(jnp.float32)
    )
    input_grad = (middle_grad + input_norm_grad).reshape(sequences, local_len, model_width)
    small = (
        grad_first_gain,
        grad_first_shift,
        grad_query_shift,
        grad_value_shift,
        grad_out_shift,
        grad_second_gain,
        grad_second_shift,
        grad_down_shift,
        grad_up_shift,
    )
    packed = jnp.concatenate([member.reshape(members, -1) for member in small], axis=1)
    summed_small = comm.reduce_small(packed)
    totals, position = [], 0
    for member in small:
        totals.append(summed_small[position : position + member.size // members])
        position = position + member.size // members
    return (
        block_out,
        input_grad,
        totals[0],
        totals[1],
        grad_qkv,
        totals[2],
        totals[3],
        grad_out,
        totals[4],
        totals[5],
        totals[6],
        grad_up,
        totals[8],
        grad_down,
        totals[7],
    )


def solution(mesh):
    comm, whole = AxisComm(), mesh
    if dict(mesh.shape) == {"replica": 8, "fsdp": 4}:
        comm = TorusComm()
        whole = jax.sharding.Mesh(mesh.devices.reshape(4, 2, 2, 2), ("z", "y", "x", "core"))
    sets, group = comm.sets, comm.group
    tokens, rows, vector = P(sets, group, None), P(group, None), P(group)
    placed = (
        tokens,
        vector,
        vector,
        rows,
        vector,
        vector,
        rows,
        vector,
        vector,
        vector,
        rows,
        vector,
        rows,
        vector,
        tokens,
    )
    return jax.shard_map(
        functools.partial(shards, comm),
        mesh=whole,
        in_specs=placed,
        out_specs=(
            tokens,
            tokens,
            vector,
            vector,
            rows,
            vector,
            vector,
            rows,
            vector,
            vector,
            vector,
            rows,
            vector,
            rows,
            vector,
        ),
        check_vma=False,
    )
```
